32 devices in a mesh: dom: 8 (over y, x, core), near: 4 (over z).
Axes of the slice: x: 2, y: 2, z: 4, core: 2. Of those that a mesh axis runs over, the one named last changes fastest.
Arguments:
- start_block: float32 [32768, 128], P(('dom', 'near')), may hold values from -6 to 6
- near_tiles: float32 [1536, 128, 128], P(('dom', 'near')), may hold values from -0.09375 to 0.09375
- near_src: int32 [1536], P(('dom', 'near')), may hold values from 0 to 31, as said below
- near_mask: int32 [1536], P(('dom', 'near')), may hold values 0 or 1
- far_tiles: float32 [256, 128, 128], P(('dom', 'near')), may hold values from -0.09375 to 0.09375
- far_src: int32 [256], P(('dom', 'near')), may hold values from 0 to 7
- far_mask: int32 [256], P(('dom', 'near')), may hold values 0 or 1
- bound_count: int32 [32], P(('dom', 'near')), may hold values from 1 to 128
Outputs:
- encodings: float32 [32768, 128], P(('dom', 'near'))
- rayleigh: float32 [128, 128], replicated
The draws below stay inside these ranges and needn't reach their ends.
Inputs may be any that keep to these rules, and one draw needn't show every extreme that they name: `near_src`: each partition holds 48 consecutive slots; the slot at position j among them (j from 0) lies in tile row j // 6; the first slot of each tile row reads the partition's own tile of that row; every source tile from another partition of the group is one of that partition's first 4 tiles.
All inputs are finite; a program needn't handle non-finite values. No bound on the sum of `near_mask` or of `far_mask` on one device may be relied on, other than what follows from the above.
Results may differ from the reference program's by a relative error of at most 0.0003.
Values sent between devices are 32-bit elements; how exact they have to be, the bound alone decides.
A program may use at most 64 MiB of HBM per device.

```python
import jax
import jax.numpy as jnp
from jax import lax

K = 128
TB = 128
TILES_DEV = 8
NPER = 6
NBT = 4
ITERS = 2
DEG = 3
NODES = 32768
NEAR_SLOTS = 1536
FAR_SLOTS = 256
N_DOM = 8
N_NEAR = 4
DEVICES = 32


def draw_near_src(key, part):
    total = DEVICES * NPER * TILES_DEV
    position = jnp.arange(total, dtype=jnp.int32)
    device = position // (NPER * TILES_DEV)
    slot = position % (NPER * TILES_DEV)
    tile_row = slot // NPER
    near_index = device % N_NEAR
    key_peer, key_own, key_border = jax.random.split(jax.random.fold_in(key, 17), 3)
    peer = jax.random.randint(key_peer, (total,), 0, N_NEAR, dtype=jnp.int32)
    own_tile = jax.random.randint(key_own, (total,), 0, TILES_DEV, dtype=jnp.int32)
    border_tile = jax.random.randint(key_border, (total,), 0, NBT, dtype=jnp.int32)
    chosen = jnp.where(peer == near_index, own_tile, border_tile)
    source = jnp.where(slot % NPER == 0, near_index * TILES_DEV + tile_row, peer * TILES_DEV + chosen)
    return source.astype(jnp.int32)


def touch_ends(values, key, smallest, top_value):
    dims = values.shape
    spot = [jax.random.randint(jax.random.fold_in(key, axis), (), 0, dims[axis]) for axis in range(len(dims))]
    values = values.at[tuple(spot)].set(smallest)
    longest = dims.index(max(dims))
    spot[longest] = (spot[longest] + 1) % dims[longest]
    return values.at[tuple(spot)].set(top_value)


def block_levels(own_key, extent, cuts, least, top_value):
    def one(dim, shards_of):
        steps = jax.random.uniform(jax.random.fold_in(jax.random.fold_in(own_key, 6), dim), (shards_of,), jnp.float32, least / len(cuts), top_value / len(cuts))
        return jnp.repeat(jnp.exp(steps), extent[dim] // shards_of).reshape((-1,) + (1,) * (len(extent) - dim - 1))

    gain = one(*cuts[0])
    for cut in cuts[1:]:
        gain = gain * one(*cut)
    return gain


def bell_draw(key, dims, spread, most, pieces=(), kind=jnp.bfloat16):
    array = jax.random.normal(key, dims, jnp.float32) * spread
    if len(pieces) > 0:
        array = block_levels(key, dims, pieces, -0.22, 0.18) * array
    return jnp.clip(array, min=-most, max=most).astype(kind)


def setup_inputs(seed: int = 0) -> dict:
    splits = jax.random.split(jax.random.key(seed), 9)
    return {
        "start_block": bell_draw(splits[0], (NODES, K), 1.0, 6.0, ((0, 32),), jnp.float32),
        "near_tiles": bell_draw(splits[1], (NEAR_SLOTS, TB, TB), (4 * (NPER + 1) * TB) ** -0.5, 0.09375, ((0, 32),), jnp.float32),
        "near_src": draw_near_src(jax.random.fold_in(splits[8], 71), 0),
        "near_mask": touch_ends((jax.random.randint(splits[3], (NEAR_SLOTS,), 0, 4) < 3).astype(jnp.int32), jax.random.fold_in(splits[3], 1), 0, 1),
        "far_tiles": bell_draw(splits[4], (FAR_SLOTS, TB, TB), (4 * (NPER + 1) * TB) ** -0.5, 0.09375, ((0, 32),), jnp.float32),
        "far_src": touch_ends(jax.random.randint(splits[5], (FAR_SLOTS,), 0, N_DOM), jax.random.fold_in(splits[5], 1), 0, N_DOM - 1).astype(jnp.int32),
        "far_mask": touch_ends((jax.random.randint(splits[6], (FAR_SLOTS,), 0, 4) < 3).astype(jnp.int32), jax.random.fold_in(splits[6], 1), 0, 1),
        "bound_count": touch_ends(jax.random.randint(splits[7], (DEVICES,), 1, TB + 1), jax.random.fold_in(splits[7], 1), 1, TB).astype(jnp.int32),
    }


LOWER_EDGE = 0.6
UPPER_EDGE = 2.0

def apply_all(block, near_tiles, near_src, near_mask, far_tiles, far_src, far_mask, bound_count):
    tile_rows = near_tiles.shape[1]
    width = block.shape[1]
    devices = bound_count.shape[0]
    tiles_dev = block.shape[0] // (devices * tile_rows)
    group_view = block.reshape(N_DOM, N_NEAR * tiles_dev, tile_rows, width)
    limit = (jnp.arange(tile_rows)[None, :] < bound_count[:, None]).astype(jnp.float32)
    edges = block.reshape(devices, tiles_dev, tile_rows, width)[:, 0] * limit[:, :, None]
    edges = edges.reshape(N_DOM, N_NEAR, tile_rows, width)
    own_view = block.reshape(devices, tiles_dev * tile_rows, width)

    def one_part(items):
        tiles, sources, masks, far_t, far_s, far_m, device = items
        dom_index = device // N_NEAR
        near_index = device % N_NEAR
        picked = group_view[dom_index][sources]
        products = jnp.einsum('sij,sjk->sik', tiles, picked, precision=lax.Precision.HIGHEST)
        products = products * masks.astype(jnp.float32)[:, None, None]
        near_sum = products.reshape(tiles_dev, NPER, tile_rows, width).sum(axis=1)
        far_pick = edges[far_s, near_index]
        far_sum = jnp.einsum('sij,sjk->sik', far_t, far_pick, precision=lax.Precision.HIGHEST)
        far_sum = far_sum * far_m.astype(jnp.float32)[:, None, None]
        return own_view[device] - (near_sum + far_sum).reshape(tiles_dev * tile_rows, width)
    items = (near_tiles.reshape(devices, NPER * tiles_dev, tile_rows, tile_rows), near_src.reshape(devices, -1), near_mask.reshape(devices, -1), far_tiles.reshape(devices, tiles_dev, tile_rows, tile_rows), far_src.reshape(devices, -1), far_mask.reshape(devices, -1), jnp.arange(devices, dtype=jnp.int32))
    return lax.map(one_part, items).reshape(block.shape)

def reference(start_block, near_tiles, near_src, near_mask, far_tiles, far_src, far_mask, bound_count):

    def operator(block):
        return apply_all(block, near_tiles, near_src, near_mask, far_tiles, far_src, far_mask, bound_count)
    center = (UPPER_EDGE + LOWER_EDGE) / 2.0
    half = (UPPER_EDGE - LOWER_EDGE) / 2.0
    nodes_all = start_block.shape[0]
    width = start_block.shape[1]
    current = start_block
    for iteration in range(ITERS):
        previous = current
        present = (operator(current) - center * current) / half
        for degree in range(DEG - 1):
            following = 2.0 * (operator(present) - center * present) / half - previous
            previous, present = (present, following)
        filtered = present
        gram = jnp.dot(filtered.T.astype(jnp.float32), filtered.astype(jnp.float32), precision=lax.Precision.HIGHEST, preferred_element_type=jnp.float32) / nodes_all
        lower = jnp.linalg.cholesky(gram)
        lower_inv = jax.scipy.linalg.solve_triangular(lower, jnp.eye(width, dtype=jnp.float32), lower=True)
        current = jnp.dot(filtered.astype(jnp.float32), lower_inv.T.astype(jnp.float32), precision=lax.Precision.HIGHEST, preferred_element_type=jnp.float32)
    image = operator(current)
    rayleigh = jnp.dot(current.T.astype(jnp.float32), image.astype(jnp.float32), precision=lax.Precision.HIGHEST, preferred_element_type=jnp.float32) / nodes_all
    return (current, rayleigh)
```

```python
from functools import partial

import jax
import jax.numpy as jnp
from jax import lax
from jax.experimental import pallas as pl
from jax.experimental.pallas import tpu as pltpu
from jax.sharding import PartitionSpec as P

NPER = 6
NBT = 4
ITERS = 2
DEG = 3
LOWER_EDGE = 0.6
UPPER_EDGE = 2.0
CENTER = (UPPER_EDGE + LOWER_EDGE) / 2.0
HALF = (UPPER_EDGE - LOWER_EDGE) / 2.0
OPS = ITERS * DEG + 1
MESH = pl.DeviceIdType.MESH
HIGHEST = lax.Precision.HIGHEST
F32 = jnp.float32
BF16 = jnp.bfloat16


def split(value, axis):
    high = value.astype(BF16)
    low = (value - high.astype(F32)).astype(BF16)
    return jnp.concatenate([high, low], axis=axis)


def quadrants(total):
    rows, columns = total.shape[0] // 2, total.shape[1] // 2
    return (total[:rows, :columns] + total[rows:, :columns]) + (
        total[:rows, columns:] + total[rows:, columns:]
    )


def inner(left, right):
    total = lax.dot_general(
        split(left, 1), split(right, 1), (((0,), (0,)), ((), ())), preferred_element_type=F32
    )
    return quadrants(total)


def times_transposed(block, factor):
    return lax.dot_general(
        block, factor, (((1,), (1,)), ((), ())), precision=HIGHEST, preferred_element_type=F32
    )


def factor_steps(gram, out_ref, per_yield):
    size = gram.shape[0]
    rows = lax.broadcasted_iota(jnp.int32, (size, size), 0)
    lanes = lax.broadcasted_iota(jnp.int32, (size, size), 1)
    right = jnp.where(rows == lanes, 1.0, 0.0).astype(F32)
    left = gram
    base = 0
    for j in range(size):
        if j - base == 8:
            left, right = left[8:], right[8:]
            base = j
        at = j - base
        row = left[at : at + 1, :]
        root = lax.rsqrt(row[:, j : j + 1])
        row_right = right[at : at + 1, :] * root
        column = left[:, j : j + 1] * root
        out_ref[j : j + 1, :] = row_right
        if j < size - 1:
            left = left - column * (row * root)
            right = right - column * row_right
        if (j + 1) % per_yield == 0:
            yield


def kernel(
    n_dom,
    n_near,
    start_ref,
    near_ref,
    src_ref,
    mask_ref,
    far_ref,
    far_src_ref,
    far_mask_ref,
    count_ref,
    enc_ref,
    ray_ref,
    *scratch,
):
    group = scratch[:OPS]
    edge = scratch[OPS : 2 * OPS]
    (
        staged,
        weights,
        image,
        inverse_1,
        inverse_2,
        parts_out,
        parts_in,
        planes,
        gathered,
        near_recv,
        near_send,
        edge_recv,
        edge_send,
        red_in_recv,
        red_in_send,
        red_plane_recv,
        red_plane_send,
        red_out_recv,
        red_out_send,
        load_sem,
    ) = scratch[2 * OPS :]
    tiles = start_ref.shape[0]
    tile_rows, width = start_ref.shape[1], start_ref.shape[2]
    nodes_all = tiles * tile_rows * n_dom * n_near
    dom = lax.axis_index("dom")
    near = lax.axis_index("near")
    mine = near * tiles
    slices = parts_out.shape[1]
    slice_rows = parts_out.shape[2]

    loads = [
        pltpu.make_async_copy(near_ref, staged.at[pl.ds(0, tiles * NPER)], load_sem.at[0]),
        pltpu.make_async_copy(far_ref, staged.at[pl.ds(tiles * NPER, tiles)], load_sem.at[1]),
    ]
    for load in loads:
        load.start()

    barrier = pltpu.get_barrier_semaphore()
    for i in range(1, n_dom):
        pl.semaphore_signal(
            barrier, inc=1, device_id={"dom": lax.rem(dom + i, n_dom)}, device_id_type=MESH
        )
    for i in range(1, n_near):
        pl.semaphore_signal(
            barrier, inc=1, device_id={"near": lax.rem(near + i, n_near)}, device_id_type=MESH
        )
    pl.semaphore_wait(barrier, n_dom + n_near - 2)

    def near_copy(k, owner, t, step):
        place = group[k].at[owner * tiles + t]
        way = 0 if step < 0 else 1
        return pltpu.make_async_remote_copy(
            src_ref=place,
            dst_ref=place,
            send_sem=near_send.at[k % 2, way, owner * NBT + t],
            recv_sem=near_recv.at[k, owner * NBT + t],
            device_id={"near": near + step},
            device_id_type=MESH,
        )

    def send_near(k, owner, t):
        @pl.when(near < n_near - 1)
        def _():
            near_copy(k, owner, t, 1).start()

        @pl.when(near > 0)
        def _():
            near_copy(k, owner, t, -1).start()

    def edge_copy(k, i):
        place = edge[k].at[dom]
        return pltpu.make_async_remote_copy(
            src_ref=place,
            dst_ref=place,
            send_sem=edge_send.at[k % 2, i],
            recv_sem=edge_recv.at[k, dom],
            device_id={"dom": lax.rem(dom + i, n_dom)},
            device_id_type=MESH,
        )

    def send_edge(k, tile):
        rows = lax.broadcasted_iota(jnp.int32, tile.shape, 0)
        edge[k][dom] = jnp.where(rows < count_ref[0], tile, 0.0)

        @pl.loop(1, n_dom)
        def _(i):
            edge_copy(k, i).start()

    def put(k, r, tile):
        group[k][mine + r] = tile

    def exchange(k, background):
        for d in range(1, n_near):
            for t in range(NBT):

                @pl.when(near >= d)
                def _():
                    owner = near - d
                    near_copy(k, owner, t, -1).wait_recv()

                    @pl.when(near < n_near - 1)
                    def _():
                        near_copy(k, owner, t, 1).start()

                @pl.when(near + d < n_near)
                def _():
                    owner = near + d
                    near_copy(k, owner, t, 1).wait_recv()

                    @pl.when(near > 0)
                    def _():
                        near_copy(k, owner, t, -1).start()

                next(background, None)
        for _ in background:
            pass

        @pl.loop(1, n_dom)
        def _(i):
            owner = lax.rem(dom + i, n_dom)
            place = edge[k].at[owner]
            pltpu.make_async_remote_copy(
                src_ref=place,
                dst_ref=place,
                send_sem=edge_send.at[k % 2, i],
                recv_sem=edge_recv.at[k, owner],
                device_id={"dom": owner},
                device_id_type=MESH,
            ).wait_recv()

    def finish_sends(k):
        for owner in range(n_near):

            @pl.when((near >= owner) & (near < n_near - 1))
            def _():
                @pl.loop(0, NBT)
                def _(t):
                    near_copy(k, owner, t, 1).wait_send()

            @pl.when((near <= owner) & (near > 0))
            def _():
                @pl.loop(0, NBT)
                def _(t):
                    near_copy(k, owner, t, -1).wait_send()

        @pl.loop(1, n_dom)
        def _(i):
            edge_copy(k, i).wait_send()

    def apply_row(k, r):
        picked = [group[k][src_ref[r * NPER + s]] for s in range(NPER)]
        picked.append(edge[k][far_src_ref[r]])
        right = jnp.concatenate([split(tile, 1) for tile in picked], axis=0)
        total = jnp.dot(weights[r], right, preferred_element_type=F32)
        return group[k][mine + r] - quadrants(total)

    def advance(k, r):
        present = group[k][mine + r]
        moved = (apply_row(k, r) - CENTER * present) / HALF
        if k % DEG == 0:
            return moved
        return 2.0 * moved - group[k - 1][mine + r]

    def reduce_steps(at, value):
        for j in range(slices):
            parts_out[at, j] = value[j * slice_rows : (j + 1) * slice_rows]

        def owner_only(body):
            if slices == n_dom:
                body()
            else:
                pl.when(dom < slices)(body)

        def in_copy(i, owner):
            peer = lax.rem(dom + i, n_dom)
            return pltpu.make_async_remote_copy(
                src_ref=parts_out.at[at, lax.rem(peer, slices)],
                dst_ref=parts_in.at[at, owner],
                send_sem=red_in_send.at[at, i],
                recv_sem=red_in_recv.at[at, owner],
                device_id={"dom": peer},
                device_id_type=MESH,
            )

        def to_owner(i, body):
            if slices == n_dom:
                body()
            else:
                pl.when(lax.rem(dom + i, n_dom) < slices)(body)

        def plane_copy(i, owner):
            return pltpu.make_async_remote_copy(
                src_ref=planes.at[at, owner],
                dst_ref=planes.at[at, owner],
                send_sem=red_plane_send.at[at, i],
                recv_sem=red_plane_recv.at[at, owner],
                device_id={"near": lax.rem(near + i, n_near)},
                device_id_type=MESH,
            )

        def out_copy(i, owner):
            return pltpu.make_async_remote_copy(
                src_ref=gathered.at[at, owner],
                dst_ref=gathered.at[at, owner],
                send_sem=red_out_send.at[at, i],
                recv_sem=red_out_recv.at[at, owner],
                device_id={"dom": lax.rem(dom + i, n_dom)},
                device_id_type=MESH,
            )

        for i in range(1, n_dom):
            to_owner(i, lambda: in_copy(i, dom).start())
        yield

        def near_sum():
            parts_in[at, dom] = parts_out[at, lax.rem(dom, slices)]
            for i in range(1, n_dom):
                in_copy(i, lax.rem(dom + i, n_dom)).wait_recv()
            planes[at, near] = jnp.sum(parts_in[at], axis=0)
            for i in range(1, n_near):
                plane_copy(i, near).start()

        owner_only(near_sum)
        yield

        def all_sum():
            for i in range(1, n_near):
                plane_copy(i, lax.rem(near + i, n_near)).wait_recv()
            gathered[at, dom] = jnp.sum(planes[at], axis=0)
            for i in range(1, n_dom):
                out_copy(i, dom).start()

        owner_only(all_sum)
        yield
        for i in range(1, n_dom):
            owner = lax.rem(dom + i, n_dom)
            to_owner(i, lambda: out_copy(i, owner).wait_recv())
            to_owner(i, lambda: in_copy(i, dom).wait_send())
            owner_only(lambda: out_copy(i, dom).wait_send())
        for i in range(1, n_near):
            owner_only(lambda: plane_copy(i, near).wait_send())
        yield

    def reduced(at):
        return jnp.concatenate([gathered[at, j] for j in range(slices)], axis=0) * (1.0 / nodes_all)

    def own_block(k):
        first = pl.multiple_of(mine, tiles)
        return group[k][pl.ds(first, tiles)].reshape(tiles * tile_rows, width)

    def prepare_steps():
        for load in loads:
            load.wait()

        @pl.loop(0, tiles)
        def _(r):
            for s in range(NPER + 1):
                if s < NPER:
                    tile = staged[r * NPER + s] * mask_ref[r * NPER + s].astype(F32)
                else:
                    tile = staged[tiles * NPER + r] * far_mask_ref[r].astype(F32)
                weights[r, :, s * tile_rows : (s + 1) * tile_rows] = split(tile, 0)

        yield

    def background(k):
        if k == 0:
            yield from prepare_steps()
        if k == DEG:
            block = own_block(k)
            yield
            steps = reduce_steps(0, inner(block, block))
            for _ in steps:
                yield
                yield
        if k == DEG + 1:
            yield from factor_steps(reduced(0), inverse_1, 12)
        if k == OPS - 1:
            block = own_block(k)
            steps = reduce_steps(1, inner(block, block))
            for _ in steps:
                yield
                yield
            yield from factor_steps(reduced(1), inverse_2, 32)

    for r in range(tiles):
        put(0, r, start_ref[r])
        if r < NBT:
            send_near(0, mine // tiles, r)
        if r == 0:
            send_edge(0, start_ref[0])

    for k in range(OPS):
        exchange(k, background(k))
        if k > 0:
            finish_sends(k - 1)
        if k < OPS - 1:

            def step(r):
                tile = advance(k, r)
                if k == OPS - 2:
                    tile = times_transposed(tile, inverse_1[...])
                put(k + 1, r, tile)
                return tile

            send_edge(k + 1, step(0))
            send_near(k + 1, near, 0)

            @pl.loop(1, NBT)
            def _(r):
                step(r)
                send_near(k + 1, near, r)

            @pl.loop(NBT, tiles)
            def _(r):
                step(r)

        else:

            @pl.loop(0, tiles)
            def _(r):
                image[r] = apply_row(k, r)

    finish_sends(OPS - 1)
    last = own_block(OPS - 1)
    steps = reduce_steps(2, inner(last, image[...].reshape(tiles * tile_rows, width)))
    next(steps)
    lower_inverse = inverse_2[...]

    @pl.loop(0, tiles)
    def _(r):
        enc_ref[r] = times_transposed(group[OPS - 1][mine + r], inverse_2[...])

    for _ in steps:
        pass
    ray_ref[...] = times_transposed(
        jnp.dot(lower_inverse, reduced(2), precision=HIGHEST, preferred_element_type=F32),
        lower_inverse,
    )


def local(
    n_dom,
    n_near,
    start_block,
    near_tiles,
    near_src,
    near_mask,
    far_tiles,
    far_src,
    far_mask,
    bound_count,
):
    tile_rows = near_tiles.shape[1]
    width = start_block.shape[1]
    tiles = start_block.shape[0] // tile_rows
    slices = min(n_dom, width // 8)
    slice_rows = width // slices
    vmem = pl.BlockSpec(memory_space=pltpu.VMEM)
    smem = pl.BlockSpec(memory_space=pltpu.SMEM)
    hbm = pl.BlockSpec(memory_space=pl.ANY)
    dma = pltpu.SemaphoreType.DMA
    scratch = [pltpu.VMEM((n_near * tiles, tile_rows, width), F32) for _ in range(OPS)]
    scratch += [pltpu.VMEM((n_dom, tile_rows, width), F32) for _ in range(OPS)]
    scratch += [
        pltpu.VMEM((tiles * (NPER + 1), tile_rows, tile_rows), F32),
        pltpu.VMEM((tiles, 2 * tile_rows, (NPER + 1) * tile_rows), BF16),
        pltpu.VMEM((tiles, tile_rows, width), F32),
        pltpu.VMEM((width, width), F32),
        pltpu.VMEM((width, width), F32),
        pltpu.VMEM((3, slices, slice_rows, width), F32),
        pltpu.VMEM((3, n_dom, slice_rows, width), F32),
        pltpu.VMEM((3, n_near, slice_rows, width), F32),
        pltpu.VMEM((3, n_dom, slice_rows, width), F32),
        dma((OPS, n_near * NBT)),
        dma((2, 2, n_near * NBT)),
        dma((OPS, n_dom)),
        dma((2, n_dom)),
        dma((3, n_dom)),
        dma((3, n_dom)),
        dma((3, n_near)),
        dma((3, n_near)),
        dma((3, n_dom)),
        dma((3, n_dom)),
        dma((2,)),
    ]
    enc, ray = pl.pallas_call(
        partial(kernel, n_dom, n_near),
        out_shape=(
            jax.ShapeDtypeStruct((tiles, tile_rows, width), F32),
            jax.ShapeDtypeStruct((width, width), F32),
        ),
        in_specs=[vmem, hbm, smem, smem, hbm, smem, smem, smem],
        out_specs=(vmem, vmem),
        scratch_shapes=scratch,
        compiler_params=pltpu.CompilerParams(
            collective_id=0, has_side_effects=True, vmem_limit_bytes=60 * 1024 * 1024
        ),
    )(
        start_block.reshape(tiles, tile_rows, width),
        near_tiles,
        near_src,
        near_mask,
        far_tiles,
        far_src,
        far_mask,
        bound_count,
    )
    return enc.reshape(start_block.shape), ray


def solution(mesh):
    shape = dict(mesh.shape)
    rows = ("dom", "near")
    return jax.shard_map(
        partial(local, shape["dom"], shape["near"]),
        mesh=mesh,
        in_specs=(
            P(rows, None),
            P(rows, None, None),
            P(rows),
            P(rows),
            P(rows, None, None),
            P(rows),
            P(rows),
            P(rows),
        ),
        out_specs=(P(rows, None), P()),
        check_vma=False,
    )
```

```python
from functools import partial

import jax
import jax.numpy as jnp
from jax import lax
from jax.experimental import pallas as pl
from jax.experimental.pallas import tpu as pltpu
from jax.sharding import PartitionSpec as P

NPER = 6
NBT = 4
ITERS = 2
DEG = 3
LOWER_EDGE = 0.6
UPPER_EDGE = 2.0
CENTER = (UPPER_EDGE + LOWER_EDGE) / 2.0
HALF = (UPPER_EDGE - LOWER_EDGE) / 2.0
OPS = ITERS * DEG + 1
MESH = pl.DeviceIdType.MESH
HIGHEST = lax.Precision.HIGHEST
F32 = jnp.float32
BF16 = jnp.bfloat16


def split(value, axis):
    high = value.astype(BF16)
    low = (value - high.astype(F32)).astype(BF16)
    return jnp.concatenate([high, low], axis=axis)


def quadrants(total):
    rows, columns = total.shape[0] // 2, total.shape[1] // 2
    return (total[:rows, :columns] + total[rows:, :columns]) + (
        total[:rows, columns:] + total[rows:, columns:]
    )


def inner(left, right):
    total = lax.dot_general(
        split(left, 1), split(right, 1), (((0,), (0,)), ((), ())), preferred_element_type=F32
    )
    return quadrants(total)


def times_transposed(block, factor):
    return lax.dot_general(
        block, factor, (((1,), (1,)), ((), ())), precision=HIGHEST, preferred_element_type=F32
    )


def factor_steps(gram, out_ref, per_yield):
    size = gram.shape[0]
    rows = lax.broadcasted_iota(jnp.int32, (size, size), 0)
    lanes = lax.broadcasted_iota(jnp.int32, (size, size), 1)
    right = jnp.where(rows == lanes, 1.0, 0.0).astype(F32)
    left = gram
    base = 0
    for j in range(size):
        if j - base == 8:
            left, right = left[8:], right[8:]
            base = j
        at = j - base
        row = left[at : at + 1, :]
        root = lax.rsqrt(row[:, j : j + 1])
        row_right = right[at : at + 1, :] * root
        column = left[:, j : j + 1] * root
        out_ref[j : j + 1, :] = row_right
        if j < size - 1:
            left = left - column * (row * root)
            right = right - column * row_right
        if (j + 1) % per_yield == 0:
            yield


def kernel(
    n_dom,
    n_near,
    start_ref,
    near_ref,
    src_ref,
    mask_ref,
    far_ref,
    far_src_ref,
    far_mask_ref,
    count_ref,
    enc_ref,
    ray_ref,
    *scratch,
):
    group = scratch[:OPS]
    edge = scratch[OPS : 2 * OPS]
    (
        staged,
        weights,
        image,
        inverse_1,
        inverse_2,
        parts_out,
        parts_in,
        planes,
        gathered,
        near_recv,
        near_send,
        edge_recv,
        edge_send,
        red_in_recv,
        red_in_send,
        red_plane_recv,
        red_plane_send,
        red_out_recv,
        red_out_send,
        load_sem,
    ) = scratch[2 * OPS :]
    tiles = start_ref.shape[0]
    tile_rows, width = start_ref.shape[1], start_ref.shape[2]
    nodes_all = tiles * tile_rows * n_dom * n_near
    dom = lax.axis_index("dom")
    near = lax.axis_index("near")
    mine = near * tiles
    slices = parts_out.shape[1]
    slice_rows = parts_out.shape[2]

    loads = [
        pltpu.make_async_copy(near_ref, staged.at[pl.ds(0, tiles * NPER)], load_sem.at[0]),
        pltpu.make_async_copy(far_ref, staged.at[pl.ds(tiles * NPER, tiles)], load_sem.at[1]),
    ]
    for load in loads:
        load.start()

    barrier = pltpu.get_barrier_semaphore()
    for i in range(1, n_dom):
        pl.semaphore_signal(
            barrier, inc=1, device_id={"dom": lax.rem(dom + i, n_dom)}, device_id_type=MESH
        )
    for i in range(1, n_near):
        pl.semaphore_signal(
            barrier, inc=1, device_id={"near": lax.rem(near + i, n_near)}, device_id_type=MESH
        )
    pl.semaphore_wait(barrier, n_dom + n_near - 2)

    def near_copy(k, owner, t, step):
        place = group[k].at[owner * tiles + t]
        way = 0 if step < 0 else 1
        return pltpu.make_async_remote_copy(
            src_ref=place,
            dst_ref=place,
            send_sem=near_send.at[k % 2, way, owner * NBT + t],
            recv_sem=near_recv.at[k, owner * NBT + t],
            device_id={"near": near + step},
            device_id_type=MESH,
        )

    def send_near(k, owner, t):
        @pl.when(near < n_near - 1)
        def _():
            near_copy(k, owner, t, 1).start()

        @pl.when(near > 0)
        def _():
            near_copy(k, owner, t, -1).start()

    def edge_copy(k, i):
        place = edge[k].at[dom]
        return pltpu.make_async_remote_copy(
            src_ref=place,
            dst_ref=place,
            send_sem=edge_send.at[k % 2, i],
            recv_sem=edge_recv.at[k, dom],
            device_id={"dom": lax.rem(dom + i, n_dom)},
            device_id_type=MESH,
        )

    def send_edge(k, tile):
        rows = lax.broadcasted_iota(jnp.int32, tile.shape, 0)
        edge[k][dom] = jnp.where(rows < count_ref[0], tile, 0.0)

        @pl.loop(1, n_dom)
        def _(i):
            edge_copy(k, i).start()

    def put(k, r, tile):
        group[k][mine + r] = tile

    def forward(k, owner, t):
        @pl.when((owner < near) & (near < n_near - 1))
        def _():
            near_copy(k, owner, t, -1).wait_recv()
            near_copy(k, owner, t, 1).start()

        @pl.when((owner > near) & (near > 0))
        def _():
            near_copy(k, owner, t, 1).wait_recv()
            near_copy(k, owner, t, -1).start()

    def exchange(k, hooks):
        pairs = (n_near + 1) // 2
        upper = near >= n_near // 2
        for d in range(1, n_near):
            for t in range(NBT):

                @pl.when(near >= d)
                def _():
                    forward(k, near - d, t)

                @pl.when(near + d < n_near)
                def _():
                    forward(k, near + d, t)

                if d == 2 and t == 1:
                    hooks["late"]()
            if d == 1:
                hooks["middle"]()
        hooks["end"]()

        @pl.when(near == 0)
        def _():
            @pl.loop(NBT, n_near * NBT)
            def _(i):
                near_copy(k, i // NBT, lax.rem(i, NBT), 1).wait_recv()

        @pl.when(near == n_near - 1)
        def _():
            @pl.loop(0, (n_near - 1) * NBT)
            def _(i):
                near_copy(k, i // NBT, lax.rem(i, NBT), -1).wait_recv()

        @pl.loop(1, n_dom)
        def _(i):
            owner = lax.rem(dom + i, n_dom)
            place = edge[k].at[owner]
            pltpu.make_async_remote_copy(
                src_ref=place,
                dst_ref=place,
                send_sem=edge_send.at[k % 2, i],
                recv_sem=edge_recv.at[k, owner],
                device_id={"dom": owner},
                device_id_type=MESH,
            ).wait_recv()

    def finish_sends(k):
        for owner in range(n_near):

            @pl.when((near >= owner) & (near < n_near - 1))
            def _():
                @pl.loop(0, NBT)
                def _(t):
                    near_copy(k, owner, t, 1).wait_send()

            @pl.when((near <= owner) & (near > 0))
            def _():
                @pl.loop(0, NBT)
                def _(t):
                    near_copy(k, owner, t, -1).wait_send()

        @pl.loop(1, n_dom)
        def _(i):
            edge_copy(k, i).wait_send()

    def apply_row(k, r):
        picked = [group[k][src_ref[r * NPER + s]] for s in range(NPER)]
        picked.append(edge[k][far_src_ref[r]])
        right = jnp.concatenate([split(tile, 1) for tile in picked], axis=0)
        total = jnp.dot(weights[r], right, preferred_element_type=F32)
        return group[k][mine + r] - quadrants(total)

    def advance(k, r):
        present = group[k][mine + r]
        moved = (apply_row(k, r) - CENTER * present) / HALF
        if k % DEG == 0:
            return moved
        return 2.0 * moved - group[k - 1][mine + r]

    def reduce_steps(at, value):
        for j in range(slices):
            parts_out[at, j] = value[j * slice_rows : (j + 1) * slice_rows]

        def owner_only(body):
            if slices == n_dom:
                body()
            else:
                pl.when(dom < slices)(body)

        def in_copy(i, owner):
            peer = lax.rem(dom + i, n_dom)
            return pltpu.make_async_remote_copy(
                src_ref=parts_out.at[at, lax.rem(peer, slices)],
                dst_ref=parts_in.at[at, owner],
                send_sem=red_in_send.at[at, i],
                recv_sem=red_in_recv.at[at, owner],
                device_id={"dom": peer},
                device_id_type=MESH,
            )

        def to_owner(i, body):
            if slices == n_dom:
                body()
            else:
                pl.when(lax.rem(dom + i, n_dom) < slices)(body)

        def plane_copy(i, owner):
            return pltpu.make_async_remote_copy(
                src_ref=planes.at[at, owner],
                dst_ref=planes.at[at, owner],
                send_sem=red_plane_send.at[at, i],
                recv_sem=red_plane_recv.at[at, owner],
                device_id={"near": lax.rem(near + i, n_near)},
                device_id_type=MESH,
            )

        def out_copy(i, owner):
            return pltpu.make_async_remote_copy(
                src_ref=gathered.at[at, owner],
                dst_ref=gathered.at[at, owner],
                send_sem=red_out_send.at[at, i],
                recv_sem=red_out_recv.at[at, owner],
                device_id={"dom": lax.rem(dom + i, n_dom)},
                device_id_type=MESH,
            )

        for i in range(1, n_dom):
            to_owner(i, lambda: in_copy(i, dom).start())
        yield

        def near_sum():
            parts_in[at, dom] = parts_out[at, lax.rem(dom, slices)]
            for i in range(1, n_dom):
                in_copy(i, lax.rem(dom + i, n_dom)).wait_recv()
            planes[at, near] = jnp.sum(parts_in[at], axis=0)
            for i in range(1, n_near):
                plane_copy(i, near).start()

        owner_only(near_sum)
        yield

        def all_sum():
            for i in range(1, n_near):
                plane_copy(i, lax.rem(near + i, n_near)).wait_recv()
            gathered[at, dom] = jnp.sum(planes[at], axis=0)
            for i in range(1, n_dom):
                out_copy(i, dom).start()

        owner_only(all_sum)
        yield
        for i in range(1, n_dom):
            owner = lax.rem(dom + i, n_dom)
            to_owner(i, lambda: out_copy(i, owner).wait_recv())
            to_owner(i, lambda: in_copy(i, dom).wait_send())
            owner_only(lambda: out_copy(i, dom).wait_send())
        for i in range(1, n_near):
            owner_only(lambda: plane_copy(i, near).wait_send())
        yield

    def reduced(at):
        return jnp.concatenate([gathered[at, j] for j in range(slices)], axis=0) * (1.0 / nodes_all)

    def own_block(k):
        first = pl.multiple_of(mine, tiles)
        return group[k][pl.ds(first, tiles)].reshape(tiles * tile_rows, width)

    def prepare():
        for load in loads:
            load.wait()

        @pl.loop(0, tiles)
        def _(r):
            for s in range(NPER + 1):
                if s < NPER:
                    tile = staged[r * NPER + s] * mask_ref[r * NPER + s].astype(F32)
                else:
                    tile = staged[tiles * NPER + r] * far_mask_ref[r].astype(F32)
                weights[r, :, s * tile_rows : (s + 1) * tile_rows] = split(tile, 0)

    running = {}

    def go_on(name):
        return lambda: next(running[name], None)

    def begin_reduce(at, k):
        block = own_block(k)
        running[at] = reduce_steps(at, inner(block, block))
        next(running[at])

    def begin_factor(at, out_ref, per_yield):
        next(running[at])
        running["factor"] = factor_steps(reduced(at), out_ref, per_yield)
        next(running["factor"])

    def hooks_of(k):
        hooks = {name: lambda: None for name in ("middle", "late", "end")}
        if k == DEG or k == OPS - 1:
            at = 0 if k == DEG else 1
            begin_reduce(at, k)
            hooks["middle"] = go_on(at)
            hooks["late"] = go_on(at)
        if k == 0:
            hooks["middle"] = prepare
        if k == DEG + 1:
            hooks["end"] = lambda: begin_factor(0, inverse_1, width // 2)
        if k == DEG + 2:
            hooks["end"] = go_on("factor")
        if k == OPS - 1:
            hooks["end"] = lambda: begin_factor(1, inverse_2, width)
        return hooks

    for r in range(tiles):
        put(0, r, start_ref[r])
        if r < NBT:
            send_near(0, mine // tiles, r)
        if r == 0:
            send_edge(0, start_ref[0])

    for k in range(OPS):
        exchange(k, hooks_of(k))
        if k > 0:
            finish_sends(k - 1)
        if k < OPS - 1:

            def step(r):
                tile = advance(k, r)
                if k == OPS - 2:
                    tile = times_transposed(tile, inverse_1[...])
                put(k + 1, r, tile)
                return tile

            send_edge(k + 1, step(0))
            send_near(k + 1, near, 0)

            @pl.loop(1, NBT)
            def _(r):
                step(r)
                send_near(k + 1, near, r)

            @pl.loop(NBT, tiles)
            def _(r):
                step(r)

        else:

            @pl.loop(0, tiles)
            def _(r):
                image[r] = apply_row(k, r)

    finish_sends(OPS - 1)
    last = own_block(OPS - 1)
    steps = reduce_steps(2, inner(last, image[...].reshape(tiles * tile_rows, width)))
    next(steps)
    lower_inverse = inverse_2[...]

    @pl.loop(0, tiles)
    def _(r):
        enc_ref[r] = times_transposed(group[OPS - 1][mine + r], inverse_2[...])

    for _ in steps:
        pass
    ray_ref[...] = times_transposed(
        jnp.dot(lower_inverse, reduced(2), precision=HIGHEST, preferred_element_type=F32),
        lower_inverse,
    )


def local(
    n_dom,
    n_near,
    start_block,
    near_tiles,
    near_src,
    near_mask,
    far_tiles,
    far_src,
    far_mask,
    bound_count,
):
    tile_rows = near_tiles.shape[1]
    width = start_block.shape[1]
    tiles = start_block.shape[0] // tile_rows
    slices = min(n_dom, width // 8)
    slice_rows = width // slices
    vmem = pl.BlockSpec(memory_space=pltpu.VMEM)
    smem = pl.BlockSpec(memory_space=pltpu.SMEM)
    hbm = pl.BlockSpec(memory_space=pl.ANY)
    dma = pltpu.SemaphoreType.DMA
    scratch = [pltpu.VMEM((n_near * tiles, tile_rows, width), F32) for _ in range(OPS)]
    scratch += [pltpu.VMEM((n_dom, tile_rows, width), F32) for _ in range(OPS)]
    scratch += [
        pltpu.VMEM((tiles * (NPER + 1), tile_rows, tile_rows), F32),
        pltpu.VMEM((tiles, 2 * tile_rows, (NPER + 1) * tile_rows), BF16),
        pltpu.VMEM((tiles, tile_rows, width), F32),
        pltpu.VMEM((width, width), F32),
        pltpu.VMEM((width, width), F32),
        pltpu.VMEM((3, slices, slice_rows, width), F32),
        pltpu.VMEM((3, n_dom, slice_rows, width), F32),
        pltpu.VMEM((3, n_near, slice_rows, width), F32),
        pltpu.VMEM((3, n_dom, slice_rows, width), F32),
        dma((OPS, n_near * NBT)),
        dma((2, 2, n_near * NBT)),
        dma((OPS, n_dom)),
        dma((2, n_dom)),
        dma((3, n_dom)),
        dma((3, n_dom)),
        dma((3, n_near)),
        dma((3, n_near)),
        dma((3, n_dom)),
        dma((3, n_dom)),
        dma((2,)),
    ]
    enc, ray = pl.pallas_call(
        partial(kernel, n_dom, n_near),
        out_shape=(
            jax.ShapeDtypeStruct((tiles, tile_rows, width), F32),
            jax.ShapeDtypeStruct((width, width), F32),
        ),
        in_specs=[vmem, hbm, smem, smem, hbm, smem, smem, smem],
        out_specs=(vmem, vmem),
        scratch_shapes=scratch,
        compiler_params=pltpu.CompilerParams(
            collective_id=0, has_side_effects=True, vmem_limit_bytes=60 * 1024 * 1024
        ),
    )(
        start_block.reshape(tiles, tile_rows, width),
        near_tiles,
        near_src,
        near_mask,
        far_tiles,
        far_src,
        far_mask,
        bound_count,
    )
    return enc.reshape(start_block.shape), ray


def solution(mesh):
    shape = dict(mesh.shape)
    rows = ("dom", "near")
    return jax.shard_map(
        partial(local, shape["dom"], shape["near"]),
        mesh=mesh,
        in_specs=(
            P(rows, None),
            P(rows, None, None),
            P(rows),
            P(rows),
            P(rows, None, None),
            P(rows),
            P(rows),
            P(rows),
        ),
        out_specs=(P(rows, None), P()),
        check_vma=False,
    )
```
